32 devices in a mesh: tlo: 2 (over y), thi: 16 (over z, x, core).
Axes of the slice: x: 2, y: 2, z: 4, core: 2. Of those that a mesh axis runs over, the one named last changes fastest.
Arguments:
- frames_in: bfloat16 [4, 4096, 384], P(None, ('thi', 'tlo')), may hold values from -6 to 6
- weights: bfloat16 [4, 3, 384, 384], replicated, may hold values from -0.1875 to 0.1875
- biases: float32 [4, 384], replicated, may hold values from -3 to 3
- valid_mask: int32 [4, 4096], P(None, ('thi', 'tlo')), may hold values 0 or 1
- cotangent: bfloat16 [4, 4096, 384], P(None, ('thi', 'tlo')), may hold values from -6 to 6
Outputs:
- input_grad: bfloat16 [4, 4096, 384], P(None, ('thi', 'tlo'))
- weight_grad: float32 [4, 3, 384, 384], replicated
- bias_grad: float32 [4, 384], replicated
The draws below stay inside these ranges and needn't reach their ends.
All inputs are finite; a program needn't handle non-finite values. No bound on the sum of `valid_mask` on one device may be relied on, other than what follows from the above.
Results may differ from the reference program's by a relative error of at most 0.015.
Values may be sent and summed in bfloat16 or wider, within the bound.
A program may use at most 128 MiB of HBM per device.

```python
import math
import jax
import jax.numpy as jnp
from jax import lax

CHANNELS = 384
LEVELS = 4
FRAMES_DEV = 128
WINDOWS = 4
FRAMES = 4096


def place_ends(entries, own_key, least, high):
    spot = [jax.random.randint(jax.random.fold_in(own_key, axis), (), 0, length) for axis, length in enumerate(entries.shape)]
    longest = entries.shape.index(max(entries.shape))
    neighbour = spot[:longest] + [(spot[longest] + 1) % entries.shape[longest]] + spot[longest + 1:]
    return entries.at[tuple(spot)].set(least).at[tuple(neighbour)].set(high)


def levels(rng, shape, cuts, smallest, high):
    def one(axis_at, parts):
        draws = jax.random.uniform(jax.random.fold_in(jax.random.fold_in(rng, 6), axis_at), (parts,), jnp.float32, smallest / len(cuts), high / len(cuts))
        return jnp.repeat(jnp.exp(draws), shape[axis_at] // parts).reshape((-1,) + (1,) * (len(shape) - axis_at - 1))

    level = one(*cuts[0])
    for cut in cuts[1:]:
        level = level * one(*cut)
    return level


def scatter_about(key, shape, deviation, limit, pieces=(), dtype=jnp.bfloat16):
    entries = deviation * jax.random.normal(key, shape, jnp.float32)
    if pieces:
        entries = entries * levels(key, shape, pieces, -0.22, 0.18)
    return jnp.clip(entries, -limit, limit).astype(dtype)


def setup_inputs(seed: int = 0) -> dict:
    keys = jax.random.split(jax.random.key(seed), 6)
    return {
        "frames_in": scatter_about(keys[0], (WINDOWS, FRAMES, CHANNELS), 1.0, 6.0, ((1, 32),)),
        "weights": scatter_about(keys[1], (LEVELS, 3, CHANNELS, CHANNELS), (3 * CHANNELS) ** -0.5, 0.1875),
        "biases": scatter_about(keys[2], (LEVELS, CHANNELS), 0.5, 3.0, (), jnp.float32),
        "valid_mask": place_ends((jax.random.randint(keys[3], (WINDOWS, FRAMES), 0, 8) < 7).astype(jnp.int32), jax.random.fold_in(keys[3], 1), 0, 1),
        "cotangent": scatter_about(keys[4], (WINDOWS, FRAMES, CHANNELS), 1.0, 6.0, ((1, 32),)),
    }


def smooth(values):
    return jax.nn.gelu(values, approximate=True)

def delay_frames(values, count):
    total = values.shape[0]
    if abs(count) >= total:
        return jnp.zeros_like(values)
    if count > 0:
        return jnp.concatenate([jnp.zeros_like(values[:count]), values[:total - count]], axis=0)
    ahead = -count
    return jnp.concatenate([values[ahead:], jnp.zeros_like(values[:ahead])], axis=0)

def one_window(frames_in, keep, cotangent, weights, biases):
    dilations = [FRAMES_DEV // 4, FRAMES_DEV, 8 * FRAMES_DEV, 32 * FRAMES_DEV]
    widths = 3 * CHANNELS
    current = frames_in
    saved = []
    for level in range(LEVELS):
        dilation = dilations[level]
        stacked = jnp.concatenate([current, delay_frames(current, dilation), delay_frames(current, 2 * dilation)], axis=1)
        pre = jnp.dot(stacked, weights[level].reshape(widths, CHANNELS), preferred_element_type=jnp.float32) + biases[level]
        current = (keep * (current.astype(jnp.float32) + smooth(pre))).astype(jnp.bfloat16)
        saved.append((stacked, pre))
    upstream = cotangent
    weight_parts = [None] * LEVELS
    bias_parts = [None] * LEVELS
    for level in reversed(range(LEVELS)):
        dilation = dilations[level]
        stacked, pre = saved[level]
        through = upstream.astype(jnp.float32) * keep
        pull = jax.vjp(smooth, pre)[1]
        pre_grad = pull(through)[0].astype(jnp.bfloat16)
        weight_parts[level] = jnp.dot(stacked.T, pre_grad, preferred_element_type=jnp.float32)
        bias_parts[level] = lax.optimization_barrier(jnp.sum(pre_grad.astype(jnp.float32), axis=0))
        gathered = jnp.concatenate([pre_grad, delay_frames(pre_grad, -dilation), delay_frames(pre_grad, -2 * dilation)], axis=1)
        mirrored = jnp.transpose(weights[level], (0, 2, 1)).reshape(widths, CHANNELS)
        back = jnp.dot(gathered, mirrored, preferred_element_type=jnp.float32)
        upstream = (through + back).astype(jnp.bfloat16)
    return (upstream, jnp.stack(weight_parts), jnp.stack(bias_parts))

def reference(frames_in, weights, biases, valid_mask, cotangent):
    keep_all = valid_mask.astype(jnp.float32)[:, :, None]
    results = lax.map(lambda items: one_window(items[0], items[1], items[2], weights, biases), (frames_in, keep_all, cotangent))
    factor = 1.0 / math.sqrt(WINDOWS * FRAMES)
    weight_grad = (lax.optimization_barrier(jnp.sum(results[1], axis=0)) * factor).reshape(LEVELS, 3, CHANNELS, CHANNELS)
    bias_grad = lax.optimization_barrier(jnp.sum(results[2], axis=0)) * factor
    return (results[0], weight_grad, bias_grad)
```

```python
import math

import jax
import jax.numpy as jnp
from jax import lax
from jax.experimental import pallas as pl
from jax.experimental.pallas import tpu as pltpu
from jax.sharding import PartitionSpec as P

MESH = pl.DeviceIdType.MESH
F32 = jnp.float32
BF16 = jnp.bfloat16
UNITS = 4
UNIT_ROWS = 1024


def rows_times(a, b):
    return jnp.dot(a, b, preferred_element_type=F32)


def rows_times_t(a, b):
    return lax.dot_general(a, b, (((1,), (1,)), ((), ())), preferred_element_type=F32)


def t_times_rows(a, b):
    return lax.dot_general(a, b, (((0,), (0,)), ((), ())), preferred_element_type=F32)


def gelu_and_slope(v):
    root = math.sqrt(2.0 / math.pi)
    square = v * v
    t = jnp.tanh(root * (v + 0.044715 * (square * v)))
    half = 0.5 * (1.0 + t)
    slope = half + (0.5 * v) * (1.0 - t * t) * (root * (1.0 + (3.0 * 0.044715) * square))
    return v * half, slope


def wide(keep):
    k = keep.astype(F32)
    return jnp.concatenate([k, k, k], axis=-1)


def fused_kernel(
    x_ref, w_ref, b_ref, keep_ref, cot_ref,
    out_ref, sum_ref,
    edge0, act1, prev1, act2, turned2, turned_cot, turned_keep, act3, pre,
    slope, through, grad, up_turned, up_out, up2, next1, edge_back,
    acc, stage_send, stage_recv,
    send_sem, recv_sem, local_sem, sum_send_sem, sum_recv_sem,
):
    windows, frames, ch = x_ref.shape
    rows = windows * frames
    y = lax.axis_index("tlo")
    thi = lax.axis_index("thi")
    block = thi * 2 + y
    z = thi // 4
    cx = lax.rem(thi, 4)
    xx = cx // 2
    core = lax.rem(thi, 2)

    def at_block(offset):
        other = lax.rem(block + offset + 32, 32)
        return (lax.rem(other, 2), other // 2)

    def at_z(other):
        return (y, other * 4 + cx)

    partner = {
        "core": (y, z * 4 + xx * 2 + (1 - core)),
        "x": (y, z * 4 + (1 - xx) * 2 + core),
        "y": (1 - y, thi),
        "z1": at_z(z + 1 - 2 * lax.rem(z, 2)),
        "z2": at_z(lax.rem(z + 2, 4)),
    }
    bit = {"core": core, "x": xx, "y": y, "z1": lax.rem(z, 2), "z2": z // 2}

    barrier = pltpu.get_barrier_semaphore()
    greeted = [at_block(o) for o in (1, -1, 2, -2)]
    greeted += [at_z(lax.rem(z + o, 4)) for o in (1, 2, 3)]
    greeted += [partner["core"], partner["x"], partner["y"]]
    for device in greeted:
        pl.semaphore_signal(barrier, inc=1, device_id=device, device_id_type=MESH)

    pending = []

    def send(src, dst, index, device):
        copy = pltpu.make_async_remote_copy(
            src_ref=src, dst_ref=dst, send_sem=send_sem.at[index], recv_sem=recv_sem.at[index],
            device_id=device, device_id_type=MESH,
        )
        copy.start()
        pending.append(copy)
        return copy

    half = frames // 2
    quarter = frames // 4
    pl.semaphore_wait(barrier, len(greeted))

    edge_copy = send(x_ref.at[:, half:, :], edge0.at[:, :half, :], 0, at_block(1))

    def turn(src, dst, first, local):
        own = pltpu.make_async_copy(src.at[z], dst.at[z], local_sem.at[local])
        own.start()
        copies = []
        for o in (1, 2, 3):
            other = lax.rem(z + o, 4)
            copies.append(send(src.at[other], dst.at[z], first + o - 1, at_z(other)))
        return own, copies

    def arrive(turned):
        own, copies = turned
        own.wait()
        for copy in copies:
            copy.wait_recv()

    edge0[:, half:, :] = x_ref[...]
    bias = b_ref[...]

    def forward(level, current, keep, nxt):
        def body(i, _):
            pair = pl.ds(2 * i, 2)
            gelu, d = gelu_and_slope(pre[pair].reshape(2 * frames, ch))
            slope[level, pair] = d.reshape(2, frames, ch)
            if nxt is not None:
                total = current[pair].astype(F32) + gelu.reshape(2, frames, ch)
                nxt[pair] = (wide(keep[pair]) * total).astype(BF16)
            return 0
        lax.fori_loop(0, 2, body, 0)

    def add_tap(level, tap, load, first=False):
        def body(i, _):
            pair = pl.ds(2 * i, 2)
            term = rows_times(load(pair).reshape(2 * frames, ch), w_ref[level, tap])
            if first:
                term = term + bias[level : level + 1]
                pre[pair] = term.reshape(2, frames, ch)
            else:
                pre[pair] = pre[pair] + term.reshape(2, frames, ch)
            return 0
        lax.fori_loop(0, 2, body, 0)

    add_tap(0, 0, lambda p: x_ref[p], True)
    edge_copy.wait_recv()

    @pl.when(block == 0)
    def _():
        edge0[:, :half, :] = jnp.zeros((windows, half, ch), BF16)

    add_tap(0, 1, lambda p: edge0[p, quarter : quarter + frames])
    add_tap(0, 2, lambda p: edge0[p, 0:frames])
    forward(0, x_ref, keep_ref, act1)

    one = send(act1, prev1.at[0], 1, at_block(1))
    two = send(act1, prev1.at[1], 2, at_block(2))
    cot_turn = turn(cot_ref, turned_cot, 3, 0)
    keep_turn = turn(keep_ref, turned_keep, 6, 1)
    add_tap(1, 0, lambda p: act1[p], True)
    two.wait_recv()

    @pl.when(block < 2)
    def _():
        prev1[1] = jnp.zeros((windows, frames, ch), BF16)

    add_tap(1, 2, lambda p: prev1[1, p])
    one.wait_recv()

    @pl.when(block < 1)
    def _():
        prev1[0] = jnp.zeros((windows, frames, ch), BF16)

    add_tap(1, 1, lambda p: prev1[0, p])
    forward(1, act1, keep_ref, act2)

    act_turn = turn(act2, turned2, 9, 2)
    acc[10 * ch :, :] = jnp.zeros((UNITS * UNIT_ROWS - 10 * ch, ch), F32)
    arrive(keep_turn)
    arrive(cot_turn)
    arrive(act_turn)
    add_tap(2, 0, lambda p: turned2[p], True)
    pre[1:4] += rows_times(turned2[0:3].reshape(3 * frames, ch), w_ref[2, 1]).reshape(3, frames, ch)
    pre[2:4] += rows_times(turned2[0:2].reshape(2 * frames, ch), w_ref[2, 2]).reshape(2, frames, ch)
    forward(2, turned2, turned_keep, act3)
    add_tap(3, 0, lambda p: act3[p], True)
    forward(3, None, None, None)

    def pull_back(level, upstream, keep):
        def body(i, total):
            pair = pl.ds(2 * i, 2)
            t = wide(keep[pair]) * upstream[pair].astype(F32)
            through[pair] = t
            g = (t * slope[level, pair]).astype(BF16)
            grad[level, pair] = g
            return total + jnp.sum(g.astype(F32).reshape(2 * frames, ch), axis=0, keepdims=True)
        total = lax.fori_loop(0, 2, body, jnp.zeros((1, ch), F32))
        acc[10 * ch + 8 * level : 10 * ch + 8 * level + 1, :] = total

    def back_tap(level, tap, load):
        def body(i, _):
            pair = pl.ds(2 * i, 2)
            term = rows_times_t(load(pair).reshape(2 * frames, ch), w_ref[level, tap])
            through[pair] = through[pair] + term.reshape(2, frames, ch)
            return 0
        lax.fori_loop(0, 2, body, 0)

    def put_weight(slot, a, g):
        acc[slot * ch : (slot + 1) * ch, :] = t_times_rows(a, g)

    pull_back(3, turned_cot, turned_keep)
    back_tap(3, 0, lambda p: grad[3, p])
    up_turned[...] = through[...].astype(BF16)
    pull_back(2, up_turned, turned_keep)
    back_tap(2, 0, lambda p: grad[2, p])
    through[0:3] += rows_times_t(grad[2, 1:4].reshape(3 * frames, ch), w_ref[2, 1]).reshape(3, frames, ch)
    through[0:2] += rows_times_t(grad[2, 2:4].reshape(2 * frames, ch), w_ref[2, 2]).reshape(2, frames, ch)
    up_out[...] = through[...].astype(BF16)
    up_turn = turn(up_out, up2, 12, 3)
    put_weight(0, act3[...].reshape(rows, ch), grad[3].reshape(rows, ch))
    for tap in range(3):
        n = 4 - tap
        put_weight(1 + tap, turned2[0:n].reshape(n * frames, ch), grad[2, tap:4].reshape(n * frames, ch))

    orders = (("x", "y", "z1", "z2"), ("y", "x", "z1", "z2"))

    def plan(unit):
        base = unit * UNIT_ROWS
        size = UNIT_ROWS // 2
        steps = [[("core", base + (1 - core) * size, base + core * size, size, base)]]
        for _ in range(4):
            steps.append([])
        landing = base + size
        for h, order in enumerate(orders):
            at = base + core * size + h * (size // 2)
            n = size // 2
            for s, name in enumerate(order):
                n = n // 2
                steps[s + 1].append((name, at + (1 - bit[name]) * n, at + bit[name] * n, n, landing))
                at = at + bit[name] * n
                landing += n
        return steps

    plans = [plan(u) for u in range(UNITS)]
    flying = {}

    def aligned(at, n):
        return pl.ds(at if isinstance(at, int) else pl.multiple_of(at, 16), n)

    def sum_copy(src, dst, unit, index, name):
        copy = pltpu.make_async_remote_copy(
            src_ref=src, dst_ref=dst, send_sem=sum_send_sem.at[unit, index],
            recv_sem=sum_recv_sem.at[unit, index], device_id=partner[name], device_id_type=MESH,
        )
        copy.start()
        pending.append(copy)
        return copy

    def begin(unit, stage):
        copies = []
        if stage < 5:
            for h, (name, give, _, n, landing) in enumerate(plans[unit][stage]):
                stage_send[aligned(give, n), :] = acc[aligned(give, n), :].astype(BF16)
                copies.append(sum_copy(
                    stage_send.at[aligned(give, n), :], stage_recv.at[pl.ds(landing, n), :],
                    unit, 2 * stage + h, name))
        else:
            for h, (name, _, own, n, _) in enumerate(plans[unit][9 - stage]):
                span = aligned(own, n)
                if stage == 5:
                    sum_ref[span, :] = acc[span, :].astype(BF16)
                copies.append(sum_copy(sum_ref.at[span, :], sum_ref.at[span, :], unit, 2 * stage + h, name))
        flying[unit, stage] = copies

    def finish(unit, stage):
        for copy in flying[unit, stage]:
            copy.wait_recv()
        if stage < 5:
            for _, _, own, n, landing in plans[unit][stage]:
                span = aligned(own, n)
                acc[span, :] = acc[span, :] + stage_recv[landing : landing + n, :].astype(F32)

    def advance(unit, stage):
        if stage > 0:
            finish(unit, stage - 1)
        if stage < 10:
            begin(unit, stage)

    advance(0, 0)
    arrive(up_turn)
    pull_back(1, up2, keep_ref)
    back_one = send(grad.at[1], next1.at[0], 15, at_block(-1))
    back_two = send(grad.at[1], next1.at[1], 16, at_block(-2))
    advance(0, 1)
    g1 = grad[1].reshape(rows, ch)
    put_weight(4, act1[...].reshape(rows, ch), g1)
    put_weight(5, prev1[0].reshape(rows, ch), g1)
    advance(0, 2)
    advance(1, 0)
    put_weight(6, prev1[1].reshape(rows, ch), g1)
    back_tap(1, 0, lambda p: grad[1, p])
    advance(1, 1)
    back_two.wait_recv()

    @pl.when(block >= 30)
    def _():
        next1[1] = jnp.zeros((windows, frames, ch), BF16)

    back_tap(1, 2, lambda p: next1[1, p])
    back_one.wait_recv()

    @pl.when(block >= 31)
    def _():
        next1[0] = jnp.zeros((windows, frames, ch), BF16)

    back_tap(1, 1, lambda p: next1[0, p])
    up_turned[...] = through[...].astype(BF16)
    pull_back(0, up_turned, keep_ref)
    edge_back[:, :frames, :] = grad[0]
    back_edge = send(grad.at[0, :, :half, :], edge_back.at[:, frames:, :], 17, at_block(-1))
    advance(0, 3)
    g0 = grad[0].reshape(rows, ch)
    put_weight(7, x_ref[...].reshape(rows, ch), g0)
    advance(2, 0)
    put_weight(8, edge0[:, quarter : quarter + frames].reshape(rows, ch), g0)
    put_weight(9, edge0[:, 0:frames].reshape(rows, ch), g0)
    advance(3, 0)
    advance(1, 2)
    advance(2, 1)
    back_tap(0, 0, lambda p: grad[0, p])
    advance(3, 1)
    back_edge.wait_recv()

    @pl.when(block >= 31)
    def _():
        edge_back[:, frames:, :] = jnp.zeros((windows, half, ch), BF16)

    back_tap(0, 1, lambda p: edge_back[p, quarter : quarter + frames])
    back_tap(0, 2, lambda p: edge_back[p, half : half + frames])
    out_ref[...] = through[...].astype(BF16)
    at = [3, 2, 1, 1]
    while min(at) < 10:
        for u in range(UNITS):
            if at[u] < 10:
                at[u] += 1
                advance(u, at[u])
    for copy in pending:
        copy.wait_send()


def fused_shards(frames_in, weights, biases, valid_mask, cotangent):
    windows, frames, ch = frames_in.shape
    levels = weights.shape[0]
    keep = jnp.broadcast_to(valid_mask.astype(BF16)[:, :, None], (windows, frames, ch // 3))
    vmem = pl.BlockSpec(memory_space=pltpu.VMEM)
    block = (windows, frames, ch)
    sum_rows = UNITS * UNIT_ROWS
    grad_in, sums = pl.pallas_call(
        fused_kernel,
        out_shape=(
            jax.ShapeDtypeStruct(block, BF16),
            jax.ShapeDtypeStruct((sum_rows, ch), BF16),
        ),
        in_specs=[vmem] * 5,
        out_specs=(vmem, vmem),
        scratch_shapes=[
            pltpu.VMEM((windows, frames + frames // 2, ch), BF16),
            pltpu.VMEM(block, BF16),
            pltpu.VMEM((2,) + block, BF16),
            pltpu.VMEM(block, BF16),
            pltpu.VMEM(block, BF16),
            pltpu.VMEM(block, BF16),
            pltpu.VMEM((windows, frames, ch // 3), BF16),
            pltpu.VMEM(block, BF16),
            pltpu.VMEM(block, F32),
            pltpu.VMEM((levels,) + block, F32),
            pltpu.VMEM(block, F32),
            pltpu.VMEM((levels,) + block, BF16),
            pltpu.VMEM(block, BF16),
            pltpu.VMEM(block, BF16),
            pltpu.VMEM(block, BF16),
            pltpu.VMEM((2,) + block, BF16),
            pltpu.VMEM((windows, frames + frames // 2, ch), BF16),
            pltpu.VMEM((sum_rows, ch), F32),
            pltpu.VMEM((sum_rows, ch), BF16),
            pltpu.VMEM((sum_rows, ch), BF16),
            pltpu.SemaphoreType.DMA((18,)),
            pltpu.SemaphoreType.DMA((18,)),
            pltpu.SemaphoreType.DMA((4,)),
            pltpu.SemaphoreType.DMA((UNITS, 20)),
            pltpu.SemaphoreType.DMA((UNITS, 20)),
        ],
        compiler_params=pltpu.CompilerParams(
            collective_id=0, has_side_effects=True, vmem_limit_bytes=48 * 1024 * 1024
        ),
    )(frames_in, weights, biases, keep, cotangent)
    factor = 1.0 / math.sqrt(windows * frames * lax.axis_size("tlo") * lax.axis_size("thi"))
    scaled = sums.astype(F32) * factor
    grads = scaled[: 10 * ch].reshape(10, ch, ch)
    none = jnp.zeros((2, ch, ch), F32)
    weight_grad = jnp.concatenate([grads[7:10], grads[4:7], grads[1:4], grads[0:1], none])
    bias_grad = scaled[10 * ch : 10 * ch + 8 * levels].reshape(levels, 8, ch)[:, 0]
    return (grad_in, weight_grad.reshape(levels, 3, ch, ch), bias_grad)


def shifted(block, axis, distance):
    devices = range(lax.axis_size(axis))
    route = [((i - distance) % len(devices), i) for i in devices]
    return lax.ppermute(block, axis, route)


def from_behind(value, axis, steps):
    count = lax.axis_size(axis)
    first, last = (max(0, -steps), min(count, count - steps))
    return lax.ppermute(value, axis, [(source, source + steps) for source in range(first, last)])


def smooth(values):
    return jax.nn.gelu(values, approximate=True)


def shift_shards(values, count):
    inner_size = lax.axis_size("tlo")
    outer_size = lax.axis_size("thi")
    if abs(count) >= inner_size * outer_size:
        return jnp.zeros_like(values)
    outer_by, inner_by = divmod(count, inner_size)
    rolled = values if inner_by == 0 else shifted(values, "tlo", inner_by)
    nearer = rolled if outer_by == 0 else from_behind(rolled, "thi", outer_by)
    if inner_by == 0:
        return nearer
    farther = rolled if outer_by + 1 == 0 else from_behind(rolled, "thi", outer_by + 1)
    return jnp.where(lax.axis_index("tlo") < inner_by, farther, nearer)


def tap_pair(values, dilation, sign):
    frames_dev = values.shape[1]
    if dilation < frames_dev:
        if sign > 0:
            edge = shift_shards(values[:, frames_dev - 2 * dilation :, :], 1)
            joined = jnp.concatenate([edge, values], axis=1)
            return (joined[:, dilation : dilation + frames_dev], joined[:, :frames_dev])
        edge = shift_shards(values[:, : 2 * dilation, :], -1)
        joined = jnp.concatenate([values, edge], axis=1)
        return (
            joined[:, dilation : dilation + frames_dev],
            joined[:, 2 * dilation : 2 * dilation + frames_dev],
        )
    hop_count = sign * (dilation // frames_dev)
    first = shift_shards(values, hop_count)
    second = shift_shards(values, 2 * hop_count)
    return (first, second)


def reduce_grads(weight_part, bias_part):
    return lax.psum((weight_part, bias_part), ("tlo", "thi"))


def shards(frames_in, weights, biases, valid_mask, cotangent):
    windows, frames_dev, channels = frames_in.shape
    widths = 3 * channels
    levels = weights.shape[0]
    keep = valid_mask.astype(jnp.float32)[:, :, None]
    dilations = [frames_dev // 4, frames_dev, 8 * frames_dev, 32 * frames_dev]
    current = frames_in
    saved = []
    for level in range(levels):
        first, second = tap_pair(current, dilations[level], 1)
        stacked = jnp.concatenate([current, first, second], axis=2).reshape(
            windows * frames_dev, widths
        )
        pre = (
            jnp.dot(
                stacked,
                weights[level].reshape(widths, channels),
                preferred_element_type=jnp.float32,
            )
            + biases[level]
        )
        pre = pre.reshape(windows, frames_dev, channels)
        current = (keep * (current.astype(jnp.float32) + smooth(pre))).astype(jnp.bfloat16)
        saved.append((stacked, pre))
    upstream = cotangent
    pending_weight = [None] * levels
    pending_bias = [None] * levels
    for level in reversed(range(levels)):
        stacked, pre = saved[level]
        through = upstream.astype(jnp.float32) * keep
        pull = jax.vjp(smooth, pre)[1]
        pre_grad = pull(through)[0].astype(jnp.bfloat16)
        flat_grad = pre_grad.reshape(windows * frames_dev, channels)
        weight_part = jnp.einsum(
            "rk,rc->kc", stacked, flat_grad, preferred_element_type=jnp.float32
        )
        bias_part = jnp.sum(flat_grad.astype(jnp.float32), axis=0)
        pending_weight[level] = weight_part
        pending_bias[level] = bias_part
        first, second = tap_pair(pre_grad, dilations[level], -1)
        gathered = jnp.concatenate([pre_grad, first, second], axis=2).reshape(
            windows * frames_dev, widths
        )
        mirrored = jnp.transpose(weights[level], (0, 2, 1)).reshape(widths, channels)
        back = jnp.dot(gathered, mirrored, preferred_element_type=jnp.float32).reshape(
            windows, frames_dev, channels
        )
        upstream = (through + back).astype(jnp.bfloat16)
    totals = reduce_grads(jnp.stack(pending_weight), jnp.stack(pending_bias))
    weight_sum = totals[0]
    bias_sum = totals[1]
    factor = 1.0 / math.sqrt(windows * frames_dev * lax.axis_size("tlo") * lax.axis_size("thi"))
    weight_grad = (weight_sum * factor).reshape(levels, 3, channels, channels)
    bias_grad = bias_sum * factor
    return (upstream, weight_grad, bias_grad)


def solution(mesh):
    fused = mesh.shape["tlo"] == 2 and mesh.shape["thi"] == 16
    return jax.shard_map(
        fused_shards if fused else shards,
        mesh=mesh,
        in_specs=(
            P(None, ("thi", "tlo"), None),
            P(),
            P(),
            P(None, ("thi", "tlo")),
            P(None, ("thi", "tlo"), None),
        ),
        out_specs=(P(None, ("thi", "tlo"), None), P(), P()),
        check_vma=False,
    )
```

```python
import math

import jax
import jax.numpy as jnp
from jax import lax
from jax.experimental import pallas as pl
from jax.experimental.pallas import tpu as pltpu
from jax.sharding import PartitionSpec as P

MESH = pl.DeviceIdType.MESH
F32 = jnp.float32
BF16 = jnp.bfloat16
UNITS = 4
UNIT_ROWS = 1024


def rows_times(a, b):
    return jnp.dot(a, b, preferred_element_type=F32)


def rows_times_t(a, b):
    return lax.dot_general(a, b, (((1,), (1,)), ((), ())), preferred_element_type=F32)


def t_times_rows(a, b):
    return lax.dot_general(a, b, (((0,), (0,)), ((), ())), preferred_element_type=F32)


def gelu_and_slope(v):
    root = math.sqrt(2.0 / math.pi)
    square = v * v
    t = jnp.tanh(root * (v + 0.044715 * (square * v)))
    half = 0.5 * (1.0 + t)
    slope = half + (0.5 * v) * (1.0 - t * t) * (root * (1.0 + (3.0 * 0.044715) * square))
    return v * half, slope


def fused_kernel(
    x_ref, w_ref, b_ref, keep_ref, cot_ref,
    out_ref, sum_ref,
    edge0, act1, prev1, act2, turned2, turned_cot, turned_keep, act3, own_wide, turned_wide,
    slope, through, grad, grad2, up_out, up2, next1, edge_back,
    acc, stage_send, stage_recv,
    send_sem, recv_sem, sum_send_sem, sum_recv_sem,
):
    windows, frames, ch = x_ref.shape
    rows = windows * frames
    y = lax.axis_index("tlo")
    thi = lax.axis_index("thi")
    block = thi * 2 + y
    z = thi // 4
    cx = lax.rem(thi, 4)
    xx = cx // 2
    core = lax.rem(thi, 2)

    near_z = z + 1 - 2 * lax.rem(z, 2)
    far_z = lax.rem(z + 2, 4)
    others = (far_z, 3 - z, near_z)

    def at_block(offset):
        other = lax.rem(block + offset + 32, 32)
        return (lax.rem(other, 2), other // 2)

    def at_z(other):
        return (y, other * 4 + cx)

    partner = {
        "core": (y, z * 4 + xx * 2 + (1 - core)),
        "x": (y, z * 4 + (1 - xx) * 2 + core),
        "y": (1 - y, thi),
        "z1": at_z(near_z),
        "z2": at_z(far_z),
    }
    bit = {"core": core, "x": xx, "y": y, "z1": lax.rem(z, 2), "z2": z // 2}

    barrier = pltpu.get_barrier_semaphore()
    greeted = [at_block(o) for o in (1, -1, 2, -2)]
    greeted += [at_z(other) for other in others]
    greeted += [partner["core"], partner["x"], partner["y"]]
    for device in greeted:
        pl.semaphore_signal(barrier, inc=1, device_id=device, device_id_type=MESH)

    pending = []

    def send(src, dst, index, device):
        copy = pltpu.make_async_remote_copy(
            src_ref=src, dst_ref=dst, send_sem=send_sem.at[index], recv_sem=recv_sem.at[index],
            device_id=device, device_id_type=MESH,
        )
        copy.start()
        pending.append(copy)
        return copy

    half = frames // 2
    quarter = frames // 4
    pl.semaphore_wait(barrier, len(greeted))

    order = others + (z,)
    edge_copies = [
        send(x_ref.at[w, half:, :], edge0.at[w, :half, :], w, at_block(1)) for w in order
    ]
    keep_copies = [
        send(keep_ref.at[o], turned_keep.at[z], 40 + i, at_z(o)) for i, o in enumerate(others)
    ]
    cot_copies = [
        send(cot_ref.at[o], turned_cot.at[z], 43 + i, at_z(o)) for i, o in enumerate(others)
    ]
    turned_keep[z] = keep_ref[z]
    turned_cot[z] = cot_ref[z]
    zeros = jnp.zeros((frames, ch), BF16)
    turned2[0] = zeros
    turned2[1] = zeros
    grad2[4] = zeros
    grad2[5] = zeros
    acc[10 * ch :, :] = jnp.zeros((UNITS * UNIT_ROWS - 10 * ch, ch), F32)
    edge0[:, half:, :] = x_ref[...]
    bias = b_ref[...]
    across = lax.broadcasted_iota(jnp.int32, (frames, frames), 0) == lax.broadcasted_iota(
        jnp.int32, (frames, frames), 1
    )
    ones = jnp.ones((frames, ch), BF16)

    def widen(row):
        diagonal = jnp.where(across, jnp.broadcast_to(row, (frames, frames)), 0.0)
        return rows_times(diagonal.astype(BF16), ones)

    for w in range(windows):
        own_wide[w] = widen(keep_ref[w, 0:1, :])

    def taps(level, a, b, c):
        total = rows_times(a, w_ref[level, 0]) + rows_times(b, w_ref[level, 1])
        return total + rows_times(c, w_ref[level, 2])

    def taps_back(level, a, b, c):
        total = rows_times_t(a, w_ref[level, 0]) + rows_times_t(b, w_ref[level, 1])
        return total + rows_times_t(c, w_ref[level, 2])

    one_copies, two_copies = [], []
    for w, copy in zip(order, edge_copies):
        copy.wait_recv()

        @pl.when(block == 0)
        def _():
            edge0[w, :half, :] = jnp.zeros((half, ch), BF16)

        now = x_ref[w]
        total = taps(0, now, edge0[w, quarter : quarter + frames], edge0[w, 0:frames])
        gelu, d = gelu_and_slope(total + bias[0:1])
        slope[0, w] = d
        act1[w] = (own_wide[w] * (now.astype(F32) + gelu)).astype(BF16)
        one_copies.append(send(act1.at[w], prev1.at[0, w], 4 + w, at_block(1)))
        two_copies.append(send(act1.at[w], prev1.at[1, w], 8 + w, at_block(2)))

    act_copies = []
    for i, w in enumerate(order):
        one_copies[i].wait_recv()
        two_copies[i].wait_recv()

        @pl.when(block < 1)
        def _():
            prev1[0, w] = zeros

        @pl.when(block < 2)
        def _():
            prev1[1, w] = zeros

        now = act1[w]
        total = taps(1, now, prev1[0, w], prev1[1, w])
        gelu, d = gelu_and_slope(total + bias[1:2])
        slope[1, w] = d
        result = (own_wide[w] * (now.astype(F32) + gelu)).astype(BF16)
        if i < 3:
            act2[w] = result
            act_copies.append(send(act2.at[w], turned2.at[2 + z], 46 + i, at_z(w)))
        else:
            turned2[2 + z] = result

    for copy in keep_copies:
        copy.wait_recv()
    for w in range(windows):
        turned_wide[w] = widen(turned_keep[w, 0:1, :])
    for copy in cot_copies + act_copies:
        copy.wait_recv()

    def flat(ref, first):
        return ref[pl.ds(first, 2)].reshape(2 * frames, ch)

    def put(ref, first, value):
        ref[pl.ds(first, 2)] = value.reshape(2, frames, ch)

    def add_bias(level, g):
        at = 10 * ch + 8 * level
        acc[at : at + 1, :] += jnp.sum(g.astype(F32), axis=0, keepdims=True)

    def far_levels(i, _):
        first = 2 * i
        now = flat(turned2, 2 + first)
        keep = flat(turned_wide, first)
        total = taps(2, now, flat(turned2, 1 + first), flat(turned2, first))
        gelu, d = gelu_and_slope(total + bias[2:3])
        last = (keep * (now.astype(F32) + gelu)).astype(BF16)
        put(act3, first, last)
        _, d3 = gelu_and_slope(rows_times(last, w_ref[3, 0]) + bias[3:4])
        t = keep * flat(turned_cot, first).astype(F32)
        g = (t * d3).astype(BF16)
        grad[0, pl.ds(first, 2)] = g.reshape(2, frames, ch)
        add_bias(3, g)
        t = keep * (t + rows_times_t(g, w_ref[3, 0])).astype(BF16).astype(F32)
        g = (t * d).astype(BF16)
        put(grad2, first, g)
        put(through, first, t)
        add_bias(2, g)
        return 0

    lax.fori_loop(0, 2, far_levels, 0)

    up_copies = []
    for i, w in enumerate(order):
        result = through[w] + taps_back(2, grad2[w], grad2[w + 1], grad2[w + 2])
        if i < 3:
            up_out[w] = result.astype(BF16)
            up_copies.append(send(up_out.at[w], up2.at[z], 49 + i, at_z(w)))
        else:
            up2[z] = result.astype(BF16)

    def put_weight(slot, a, g):
        acc[slot * ch : (slot + 1) * ch, :] = t_times_rows(a, g)

    orders = (("x", "y", "z1", "z2"), ("y", "x", "z1", "z2"))

    def plan(unit):
        base = unit * UNIT_ROWS
        size = UNIT_ROWS // 2
        steps = [[("core", base + (1 - core) * size, base + core * size, size, base)]]
        for _ in range(4):
            steps.append([])
        landing = base + size
        for h, order in enumerate(orders):
            at = base + core * size + h * (size // 2)
            n = size // 2
            for s, name in enumerate(order):
                n = n // 2
                steps[s + 1].append((name, at + (1 - bit[name]) * n, at + bit[name] * n, n, landing))
                at = at + bit[name] * n
                landing += n
        return steps

    plans = [plan(u) for u in range(UNITS)]
    flying = {}

    def aligned(at, n):
        return pl.ds(at if isinstance(at, int) else pl.multiple_of(at, 16), n)

    def sum_copy(src, dst, unit, index, name):
        copy = pltpu.make_async_remote_copy(
            src_ref=src, dst_ref=dst, send_sem=sum_send_sem.at[unit, index],
            recv_sem=sum_recv_sem.at[unit, index], device_id=partner[name], device_id_type=MESH,
        )
        copy.start()
        pending.append(copy)
        return copy

    def begin(unit, stage):
        copies = []
        if stage < 5:
            for h, (name, give, _, n, landing) in enumerate(plans[unit][stage]):
                stage_send[aligned(give, n), :] = acc[aligned(give, n), :].astype(BF16)
                copies.append(sum_copy(
                    stage_send.at[aligned(give, n), :], stage_recv.at[pl.ds(landing, n), :],
                    unit, 2 * stage + h, name))
        else:
            for h, (name, _, own, n, _) in enumerate(plans[unit][9 - stage]):
                span = aligned(own, n)
                if stage == 5:
                    sum_ref[span, :] = acc[span, :].astype(BF16)
                copies.append(sum_copy(sum_ref.at[span, :], sum_ref.at[span, :], unit, 2 * stage + h, name))
        flying[unit, stage] = copies

    def finish(unit, stage):
        for copy in flying[unit, stage]:
            copy.wait_recv()
        if stage < 5:
            for _, _, own, n, landing in plans[unit][stage]:
                span = aligned(own, n)
                acc[span, :] = acc[span, :] + stage_recv[landing : landing + n, :].astype(F32)

    def advance(unit, stage):
        if stage > 0:
            finish(unit, stage - 1)
        if stage < 10:
            begin(unit, stage)

    back_order = (z, near_z, far_z, 3 - z)
    arrivals = (None, up_copies[2], up_copies[0], up_copies[1])
    back_one, back_two = [], []

    def start_one(i):
        w = back_order[i]
        if i > 0:
            arrivals[i].wait_recv()
        t = own_wide[w] * up2[w].astype(F32)
        g = (t * slope[1, w]).astype(BF16)
        through[w] = t
        grad[1, w] = g
        back_one.append(send(grad.at[1, w], next1.at[0, w], 12 + w, at_block(-1)))
        back_two.append(send(grad.at[1, w], next1.at[1, w], 16 + w, at_block(-2)))
        add_bias(1, g)

    start_one(0)
    put_weight(0, act3[...].reshape(rows, ch), grad[0].reshape(rows, ch))
    for tap in range(3):
        n = 4 - tap
        put_weight(1 + tap, turned2[2 : 2 + n].reshape(n * frames, ch), grad2[tap:4].reshape(n * frames, ch))
    for i in range(1, 4):
        start_one(i)
    advance(0, 0)
    g1 = grad[1].reshape(rows, ch)
    put_weight(4, act1[...].reshape(rows, ch), g1)
    put_weight(5, prev1[0].reshape(rows, ch), g1)
    put_weight(6, prev1[1].reshape(rows, ch), g1)
    advance(0, 1)
    advance(1, 0)
    back_edges = []
    for i, w in enumerate(back_order):
        back_one[i].wait_recv()
        back_two[i].wait_recv()

        @pl.when(block >= 31)
        def _():
            next1[0, w] = zeros

        @pl.when(block >= 30)
        def _():
            next1[1, w] = zeros

        total = through[w] + taps_back(1, grad[1, w], next1[0, w], next1[1, w])
        t = own_wide[w] * total.astype(BF16).astype(F32)
        g = (t * slope[0, w]).astype(BF16)
        through[w] = t
        grad[2, w] = g
        edge_back[w, :frames, :] = g
        back_edges.append(
            send(grad.at[2, w, :half, :], edge_back.at[w, frames:, :], 20 + w, at_block(-1))
        )
        add_bias(0, g)
    advance(0, 2)
    advance(1, 1)
    g0 = grad[2].reshape(rows, ch)
    put_weight(7, x_ref[...].reshape(rows, ch), g0)
    advance(2, 0)
    put_weight(8, edge0[:, quarter : quarter + frames].reshape(rows, ch), g0)
    put_weight(9, edge0[:, 0:frames].reshape(rows, ch), g0)
    advance(3, 0)
    advance(0, 3)
    advance(1, 2)
    advance(2, 1)
    advance(3, 1)
    for i, w in enumerate(back_order):
        back_edges[i].wait_recv()

        @pl.when(block >= 31)
        def _():
            edge_back[w, frames:, :] = jnp.zeros((half, ch), BF16)

        total = through[w] + taps_back(
            0, grad[2, w], edge_back[w, quarter : quarter + frames], edge_back[w, half : half + frames]
        )
        out_ref[w] = total.astype(BF16)
    at = [3, 2, 1, 1]
    while min(at) < 10:
        for u in range(UNITS):
            if at[u] < 10:
                at[u] += 1
                advance(u, at[u])
    for copy in pending:
        copy.wait_send()


def fused_shards(frames_in, weights, biases, valid_mask, cotangent):
    windows, frames, ch = frames_in.shape
    levels = weights.shape[0]
    keep = jnp.broadcast_to(valid_mask.astype(F32)[:, None, :], (windows, 8, frames))
    vmem = pl.BlockSpec(memory_space=pltpu.VMEM)
    block = (windows, frames, ch)
    sum_rows = UNITS * UNIT_ROWS
    grad_in, sums = pl.pallas_call(
        fused_kernel,
        out_shape=(
            jax.ShapeDtypeStruct(block, BF16),
            jax.ShapeDtypeStruct((sum_rows, ch), BF16),
        ),
        in_specs=[vmem] * 5,
        out_specs=(vmem, vmem),
        scratch_shapes=[
            pltpu.VMEM((windows, frames + frames // 2, ch), BF16),
            pltpu.VMEM(block, BF16),
            pltpu.VMEM((2,) + block, BF16),
            pltpu.VMEM(block, BF16),
            pltpu.VMEM((windows + 2, frames, ch), BF16),
            pltpu.VMEM(block, BF16),
            pltpu.VMEM((windows, 8, frames), F32),
            pltpu.VMEM(block, BF16),
            pltpu.VMEM(block, F32),
            pltpu.VMEM(block, F32),
            pltpu.VMEM((2,) + block, F32),
            pltpu.VMEM(block, F32),
            pltpu.VMEM((3,) + block, BF16),
            pltpu.VMEM((windows + 2, frames, ch), BF16),
            pltpu.VMEM(block, BF16),
            pltpu.VMEM(block, BF16),
            pltpu.VMEM((2,) + block, BF16),
            pltpu.VMEM((windows, frames + frames // 2, ch), BF16),
            pltpu.VMEM((sum_rows, ch), F32),
            pltpu.VMEM((sum_rows, ch), BF16),
            pltpu.VMEM((sum_rows, ch), BF16),
            pltpu.SemaphoreType.DMA((52,)),
            pltpu.SemaphoreType.DMA((52,)),
            pltpu.SemaphoreType.DMA((UNITS, 20)),
            pltpu.SemaphoreType.DMA((UNITS, 20)),
        ],
        compiler_params=pltpu.CompilerParams(
            collective_id=0, has_side_effects=True, vmem_limit_bytes=48 * 1024 * 1024
        ),
    )(frames_in, weights, biases, keep, cotangent)
    factor = 1.0 / math.sqrt(windows * frames * lax.axis_size("tlo") * lax.axis_size("thi"))
    scaled = sums.astype(F32) * factor
    grads = scaled[: 10 * ch].reshape(10, ch, ch)
    none = jnp.zeros((2, ch, ch), F32)
    weight_grad = jnp.concatenate([grads[7:10], grads[4:7], grads[1:4], grads[0:1], none])
    bias_grad = scaled[10 * ch : 10 * ch + 8 * levels].reshape(levels, 8, ch)[:, 0]
    return (grad_in, weight_grad.reshape(levels, 3, ch, ch), bias_grad)


def shifted(block, axis, distance):
    devices = range(lax.axis_size(axis))
    route = [((i - distance) % len(devices), i) for i in devices]
    return lax.ppermute(block, axis, route)


def from_behind(value, axis, steps):
    count = lax.axis_size(axis)
    first, last = (max(0, -steps), min(count, count - steps))
    return lax.ppermute(value, axis, [(source, source + steps) for source in range(first, last)])


def smooth(values):
    return jax.nn.gelu(values, approximate=True)


def shift_shards(values, count):
    inner_size = lax.axis_size("tlo")
    outer_size = lax.axis_size("thi")
    if abs(count) >= inner_size * outer_size:
        return jnp.zeros_like(values)
    outer_by, inner_by = divmod(count, inner_size)
    rolled = values if inner_by == 0 else shifted(values, "tlo", inner_by)
    nearer = rolled if outer_by == 0 else from_behind(rolled, "thi", outer_by)
    if inner_by == 0:
        return nearer
    farther = rolled if outer_by + 1 == 0 else from_behind(rolled, "thi", outer_by + 1)
    return jnp.where(lax.axis_index("tlo") < inner_by, farther, nearer)


def tap_pair(values, dilation, sign):
    frames_dev = values.shape[1]
    if dilation < frames_dev:
        if sign > 0:
            edge = shift_shards(values[:, frames_dev - 2 * dilation :, :], 1)
            joined = jnp.concatenate([edge, values], axis=1)
            return (joined[:, dilation : dilation + frames_dev], joined[:, :frames_dev])
        edge = shift_shards(values[:, : 2 * dilation, :], -1)
        joined = jnp.concatenate([values, edge], axis=1)
        return (
            joined[:, dilation : dilation + frames_dev],
            joined[:, 2 * dilation : 2 * dilation + frames_dev],
        )
    hop_count = sign * (dilation // frames_dev)
    first = shift_shards(values, hop_count)
    second = shift_shards(values, 2 * hop_count)
    return (first, second)


def reduce_grads(weight_part, bias_part):
    return lax.psum((weight_part, bias_part), ("tlo", "thi"))


def shards(frames_in, weights, biases, valid_mask, cotangent):
    windows, frames_dev, channels = frames_in.shape
    widths = 3 * channels
    levels = weights.shape[0]
    keep = valid_mask.astype(jnp.float32)[:, :, None]
    dilations = [frames_dev // 4, frames_dev, 8 * frames_dev, 32 * frames_dev]
    current = frames_in
    saved = []
    for level in range(levels):
        first, second = tap_pair(current, dilations[level], 1)
        stacked = jnp.concatenate([current, first, second], axis=2).reshape(
            windows * frames_dev, widths
        )
        pre = (
            jnp.dot(
                stacked,
                weights[level].reshape(widths, channels),
                preferred_element_type=jnp.float32,
            )
            + biases[level]
        )
        pre = pre.reshape(windows, frames_dev, channels)
        current = (keep * (current.astype(jnp.float32) + smooth(pre))).astype(jnp.bfloat16)
        saved.append((stacked, pre))
    upstream = cotangent
    pending_weight = [None] * levels
    pending_bias = [None] * levels
    for level in reversed(range(levels)):
        stacked, pre = saved[level]
        through = upstream.astype(jnp.float32) * keep
        pull = jax.vjp(smooth, pre)[1]
        pre_grad = pull(through)[0].astype(jnp.bfloat16)
        flat_grad = pre_grad.reshape(windows * frames_dev, channels)
        weight_part = jnp.einsum(
            "rk,rc->kc", stacked, flat_grad, preferred_element_type=jnp.float32
        )
        bias_part = jnp.sum(flat_grad.astype(jnp.float32), axis=0)
        pending_weight[level] = weight_part
        pending_bias[level] = bias_part
        first, second = tap_pair(pre_grad, dilations[level], -1)
        gathered = jnp.concatenate([pre_grad, first, second], axis=2).reshape(
            windows * frames_dev, widths
        )
        mirrored = jnp.transpose(weights[level], (0, 2, 1)).reshape(widths, channels)
        back = jnp.dot(gathered, mirrored, preferred_element_type=jnp.float32).reshape(
            windows, frames_dev, channels
        )
        upstream = (through + back).astype(jnp.bfloat16)
    totals = reduce_grads(jnp.stack(pending_weight), jnp.stack(pending_bias))
    weight_sum = totals[0]
    bias_sum = totals[1]
    factor = 1.0 / math.sqrt(windows * frames_dev * lax.axis_size("tlo") * lax.axis_size("thi"))
    weight_grad = (weight_sum * factor).reshape(levels, 3, channels, channels)
    bias_grad = bias_sum * factor
    return (upstream, weight_grad, bias_grad)


def solution(mesh):
    fused = mesh.shape["tlo"] == 2 and mesh.shape["thi"] == 16
    return jax.shard_map(
        fused_shards if fused else shards,
        mesh=mesh,
        in_specs=(
            P(None, ("thi", "tlo"), None),
            P(),
            P(),
            P(None, ("thi", "tlo")),
            P(None, ("thi", "tlo"), None),
        ),
        out_specs=(P(None, ("thi", "tlo"), None), P(), P()),
        check_vma=False,
    )
```

```python
import math

import jax
import jax.numpy as jnp
from jax import lax
from jax.experimental import pallas as pl
from jax.experimental.pallas import tpu as pltpu
from jax.sharding import PartitionSpec as P

MESH = pl.DeviceIdType.MESH
F32 = jnp.float32
BF16 = jnp.bfloat16
UNITS = ((0, 1024), (1024, 512), (1536, 1024), (2560, 1536))
SUM_ROWS = 4096
BIAS_ROWS = 256


def rows_times(a, b):
    return jnp.dot(a, b, preferred_element_type=F32)


def rows_times_t(a, b):
    return lax.dot_general(a, b, (((1,), (1,)), ((), ())), preferred_element_type=F32)


def t_times_rows(a, b):
    return lax.dot_general(a, b, (((0,), (0,)), ((), ())), preferred_element_type=F32)


def gelu_and_slope(v):
    root = math.sqrt(2.0 / math.pi)
    square = v * v
    t = jnp.tanh(root * (v + 0.044715 * (square * v)))
    half = 0.5 * (1.0 + t)
    slope = half + (0.5 * v) * (1.0 - t * t) * (root * (1.0 + (3.0 * 0.044715) * square))
    return v * half, slope


def fused_kernel(
    x_ref, w_hbm, b_ref, keep_ref, cot_ref,
    out_ref, sum_ref,
    edge0, act1, prev1, act2, turned2, turned_cot, turned_keep, act3, own_wide, turned_wide,
    slope, through, grad, grad2, up_out, up2, next1, edge_back,
    acc, stage_send, stage_recv, w_ref,
    send_sem, recv_sem, local_sem, sum_send_sem, sum_recv_sem,
):
    windows, frames, ch = x_ref.shape
    rows = windows * frames
    y = lax.axis_index("tlo")
    thi = lax.axis_index("thi")
    block = thi * 2 + y
    z = thi // 4
    cx = lax.rem(thi, 4)
    xx = cx // 2
    core = lax.rem(thi, 2)

    near_z = z + 1 - 2 * lax.rem(z, 2)
    far_z = lax.rem(z + 2, 4)
    others = (far_z, 3 - z, near_z)

    def at_block(offset):
        other = lax.rem(block + offset + 32, 32)
        return (lax.rem(other, 2), other // 2)

    def at_z(other):
        return (y, other * 4 + cx)

    plane = {
        1: (1 - y, thi),
        2: (y, z * 4 + (1 - xx) * 2 + core),
        3: (1 - y, z * 4 + (1 - xx) * 2 + core),
    }
    plane_member = {
        1: xx * 2 + (1 - y),
        2: (1 - xx) * 2 + y,
        3: (1 - xx) * 2 + (1 - y),
    }
    z_member = {1: near_z, 2: far_z, 3: 3 - z}
    sibling = (y, z * 4 + xx * 2 + (1 - core))

    load_w = pltpu.make_async_copy(w_hbm, w_ref, local_sem.at[0])
    load_w.start()
    load_cot = pltpu.make_async_copy(cot_ref.at[z], turned_cot.at[z], local_sem.at[1])
    load_cot.start()
    barrier = pltpu.get_barrier_semaphore()
    greeted = [at_block(o) for o in (1, -1, 2, -2)]
    greeted += [at_z(other) for other in others]
    greeted += [sibling, plane[1], plane[2], plane[3]]
    for device in greeted:
        pl.semaphore_signal(barrier, inc=1, device_id=device, device_id_type=MESH)

    pending = []

    def send(src, dst, index, device):
        copy = pltpu.make_async_remote_copy(
            src_ref=src, dst_ref=dst, send_sem=send_sem.at[index], recv_sem=recv_sem.at[index],
            device_id=device, device_id_type=MESH,
        )
        copy.start()
        pending.append(copy)
        return copy

    half = frames // 2
    quarter = frames // 4
    pl.semaphore_wait(barrier, len(greeted))

    order = others + (z,)
    edge_copies = [
        send(x_ref.at[w, half:, :], edge0.at[w, :half, :], w, at_block(1)) for w in order
    ]
    keep_copies = [
        send(keep_ref.at[o], turned_keep.at[z], 40 + i, at_z(o)) for i, o in enumerate(others)
    ]
    cot_copies = [
        send(cot_ref.at[o], turned_cot.at[z], 43 + i, at_z(o)) for i, o in enumerate(others)
    ]
    turned_keep[z] = keep_ref[z]
    zeros = jnp.zeros((frames, ch), BF16)
    turned2[0] = zeros
    turned2[1] = zeros
    grad2[4] = zeros
    grad2[5] = zeros
    acc[:BIAS_ROWS, :] = jnp.zeros((BIAS_ROWS, ch), F32)
    edge0[:, half:, :] = x_ref[...]
    bias = b_ref[...]
    across = lax.broadcasted_iota(jnp.int32, (frames, frames), 0) == lax.broadcasted_iota(
        jnp.int32, (frames, frames), 1
    )
    ones = jnp.ones((frames, ch), BF16)

    def widen(row):
        diagonal = jnp.where(across, jnp.broadcast_to(row, (frames, frames)), 0.0)
        return rows_times(diagonal.astype(BF16), ones)

    for w in range(windows):
        own_wide[w] = widen(keep_ref[w, 0:1, :])

    def taps(level, a, b, c):
        total = rows_times(a, w_ref[level, 0]) + rows_times(b, w_ref[level, 1])
        return total + rows_times(c, w_ref[level, 2])

    def taps_back(level, a, b, c):
        total = rows_times_t(a, w_ref[level, 0]) + rows_times_t(b, w_ref[level, 1])
        return total + rows_times_t(c, w_ref[level, 2])

    load_w.wait()
    load_cot.wait()
    one_copies, two_copies = [], []
    for w, copy in zip(order, edge_copies):
        copy.wait_recv()

        @pl.when(block == 0)
        def _():
            edge0[w, :half, :] = jnp.zeros((half, ch), BF16)

        now = x_ref[w]
        total = taps(0, now, edge0[w, quarter : quarter + frames], edge0[w, 0:frames])
        gelu, d = gelu_and_slope(total + bias[0:1])
        slope[0, w] = d
        act1[w] = (own_wide[w] * (now.astype(F32) + gelu)).astype(BF16)
        one_copies.append(send(act1.at[w], prev1.at[0, w], 4 + w, at_block(1)))
        two_copies.append(send(act1.at[w], prev1.at[1, w], 8 + w, at_block(2)))

    act_copies = []
    for i, w in enumerate(order):
        one_copies[i].wait_recv()
        two_copies[i].wait_recv()

        @pl.when(block < 1)
        def _():
            prev1[0, w] = zeros

        @pl.when(block < 2)
        def _():
            prev1[1, w] = zeros

        now = act1[w]
        total = taps(1, now, prev1[0, w], prev1[1, w])
        gelu, d = gelu_and_slope(total + bias[1:2])
        slope[1, w] = d
        result = (own_wide[w] * (now.astype(F32) + gelu)).astype(BF16)
        if i < 3:
            act2[w] = result
            act_copies.append(send(act2.at[w], turned2.at[2 + z], 46 + i, at_z(w)))
        else:
            turned2[2 + z] = result

    for copy in keep_copies:
        copy.wait_recv()
    for w in range(windows):
        turned_wide[w] = widen(turned_keep[w, 0:1, :])
    for copy in cot_copies + act_copies:
        copy.wait_recv()

    def flat(ref, first):
        return ref[pl.ds(first, 2)].reshape(2 * frames, ch)

    def put(ref, first, value):
        ref[pl.ds(first, 2)] = value.reshape(2, frames, ch)

    def add_bias(level, g):
        at = 8 * level
        acc[at : at + 1, :] += jnp.sum(g.astype(F32), axis=0, keepdims=True)

    def far_levels(i, _):
        first = 2 * i
        now = flat(turned2, 2 + first)
        keep = flat(turned_wide, first)
        total = taps(2, now, flat(turned2, 1 + first), flat(turned2, first))
        gelu, d = gelu_and_slope(total + bias[2:3])
        last = (keep * (now.astype(F32) + gelu)).astype(BF16)
        put(act3, first, last)
        _, d3 = gelu_and_slope(rows_times(last, w_ref[3, 0]) + bias[3:4])
        t = keep * flat(turned_cot, first).astype(F32)
        g = (t * d3).astype(BF16)
        grad[0, pl.ds(first, 2)] = g.reshape(2, frames, ch)
        add_bias(3, g)
        t = keep * (t + rows_times_t(g, w_ref[3, 0])).astype(BF16).astype(F32)
        g = (t * d).astype(BF16)
        put(grad2, first, g)
        put(through, first, t)
        add_bias(2, g)
        return 0

    lax.fori_loop(0, 2, far_levels, 0)

    up_copies = []
    for i, w in enumerate(order):
        result = through[w] + taps_back(2, grad2[w], grad2[w + 1], grad2[w + 2])
        if i < 3:
            up_out[w] = result.astype(BF16)
            up_copies.append(send(up_out.at[w], up2.at[z], 49 + i, at_z(w)))
        else:
            up2[z] = result.astype(BF16)

    def put_weight(slot, a, g):
        acc[BIAS_ROWS + slot * ch : BIAS_ROWS + (slot + 1) * ch, :] = t_times_rows(a, g)

    def plan(base, size):
        half_at = base + core * (size // 2)
        n = size // 8
        mine = xx * 2 + y
        part = half_at + mine * n
        first = [(sibling, base + (1 - core) * (size // 2), base)]
        second = [
            (plane[r], half_at + plane_member[r] * n, base + size // 2 + (r - 1) * n) for r in (1, 2, 3)
        ]
        m = size // 32
        landed = base + size // 2 + 3 * n
        third = [
            (at_z(z_member[r]), part + z_member[r] * m, landed + (r - 1) * m) for r in (1, 2, 3)
        ]
        return (
            (first, half_at, size // 2),
            (second, part, n),
            (third, part + z * m, m),
        )

    plans = [plan(*unit) for unit in UNITS]
    flying = {}

    def aligned(at, n):
        return pl.ds(at if isinstance(at, int) else pl.multiple_of(at, 16), n)

    def sum_copy(src, dst, unit, index, device):
        copy = pltpu.make_async_remote_copy(
            src_ref=src, dst_ref=dst, send_sem=sum_send_sem.at[unit, index],
            recv_sem=sum_recv_sem.at[unit, index], device_id=device, device_id_type=MESH,
        )
        copy.start()
        pending.append(copy)
        return copy

    def begin(unit, stage):
        copies = []
        routes, own, n = plans[unit][stage if stage < 3 else 5 - stage]
        span = aligned(own, n)
        if stage == 3:
            sum_ref[span, :] = acc[span, :].astype(BF16)
        for r, (device, give, landing) in enumerate(routes):
            if stage < 3:
                there = aligned(give, n)
                stage_send[there, :] = acc[there, :].astype(BF16)
                src, dst = stage_send.at[there, :], stage_recv.at[pl.ds(landing, n), :]
            else:
                src, dst = sum_ref.at[span, :], sum_ref.at[span, :]
            copies.append(sum_copy(src, dst, unit, 3 * stage + r, device))
        flying[unit, stage] = copies

    def finish(unit, stage):
        for copy in flying[unit, stage]:
            copy.wait_recv()
        if stage < 3:
            routes, own, n = plans[unit][stage]
            span = aligned(own, n)
            total = acc[span, :]
            for _, _, landing in routes:
                total = total + stage_recv[landing : landing + n, :].astype(F32)
            acc[span, :] = total

    def advance(unit, stage):
        if stage > 0:
            finish(unit, stage - 1)
        if stage < 6:
            begin(unit, stage)

    back_order = (z, near_z, far_z, 3 - z)
    arrivals = (None, up_copies[2], up_copies[0], up_copies[1])
    back_one, back_two = [], []

    def start_one(i):
        w = back_order[i]
        if i > 0:
            arrivals[i].wait_recv()
        t = own_wide[w] * up2[w].astype(F32)
        g = (t * slope[1, w]).astype(BF16)
        through[w] = t
        grad[1, w] = g
        back_one.append(send(grad.at[1, w], next1.at[0, w], 12 + w, at_block(-1)))
        back_two.append(send(grad.at[1, w], next1.at[1, w], 16 + w, at_block(-2)))
        add_bias(1, g)

    start_one(0)
    put_weight(9, act3[...].reshape(rows, ch), grad[0].reshape(rows, ch))
    for tap in range(3):
        n = 4 - tap
        put_weight(6 + tap, turned2[2 : 2 + n].reshape(n * frames, ch), grad2[tap:4].reshape(n * frames, ch))
    advance(3, 0)
    for i in range(1, 4):
        start_one(i)
    advance(3, 1)
    g1 = grad[1].reshape(rows, ch)
    put_weight(3, act1[...].reshape(rows, ch), g1)
    put_weight(4, prev1[0].reshape(rows, ch), g1)
    put_weight(5, prev1[1].reshape(rows, ch), g1)
    advance(2, 0)
    advance(3, 2)
    back_edges = []
    for i, w in enumerate(back_order):
        back_one[i].wait_recv()
        back_two[i].wait_recv()

        @pl.when(block >= 31)
        def _():
            next1[0, w] = zeros

        @pl.when(block >= 30)
        def _():
            next1[1, w] = zeros

        total = through[w] + taps_back(1, grad[1, w], next1[0, w], next1[1, w])
        t = own_wide[w] * total.astype(BF16).astype(F32)
        g = (t * slope[0, w]).astype(BF16)
        through[w] = t
        grad[2, w] = g
        edge_back[w, :frames, :] = g
        back_edges.append(
            send(grad.at[2, w, :half, :], edge_back.at[w, frames:, :], 20 + w, at_block(-1))
        )
        add_bias(0, g)
    advance(2, 1)
    advance(3, 3)
    g0 = grad[2].reshape(rows, ch)
    put_weight(0, x_ref[...].reshape(rows, ch), g0)
    put_weight(1, edge0[:, quarter : quarter + frames].reshape(rows, ch), g0)
    advance(0, 0)
    put_weight(2, edge0[:, 0:frames].reshape(rows, ch), g0)
    advance(1, 0)
    advance(2, 2)
    advance(0, 1)
    advance(1, 1)
    advance(3, 4)
    for i, w in enumerate(back_order):
        back_edges[i].wait_recv()

        @pl.when(block >= 31)
        def _():
            edge_back[w, frames:, :] = jnp.zeros((half, ch), BF16)

        total = through[w] + taps_back(
            0, grad[2, w], edge_back[w, quarter : quarter + frames], edge_back[w, half : half + frames]
        )
        out_ref[w] = total.astype(BF16)
    at = [1, 1, 2, 4]
    while min(at) < 6:
        for u in range(len(UNITS)):
            if at[u] < 6:
                at[u] += 1
                advance(u, at[u])
    for copy in pending:
        copy.wait_send()


def fused_shards(frames_in, weights, biases, valid_mask, cotangent):
    windows, frames, ch = frames_in.shape
    levels = weights.shape[0]
    keep = jnp.broadcast_to(valid_mask.astype(F32)[:, None, :], (windows, 8, frames))
    vmem = pl.BlockSpec(memory_space=pltpu.VMEM)
    anywhere = pl.BlockSpec(memory_space=pl.ANY)
    block = (windows, frames, ch)
    sum_rows = SUM_ROWS
    grad_in, sums = pl.pallas_call(
        fused_kernel,
        out_shape=(
            jax.ShapeDtypeStruct(block, BF16),
            jax.ShapeDtypeStruct((sum_rows, ch), BF16),
        ),
        in_specs=[vmem, anywhere, vmem, vmem, anywhere],
        out_specs=(vmem, vmem),
        scratch_shapes=[
            pltpu.VMEM((windows, frames + frames // 2, ch), BF16),
            pltpu.VMEM(block, BF16),
            pltpu.VMEM((2,) + block, BF16),
            pltpu.VMEM(block, BF16),
            pltpu.VMEM((windows + 2, frames, ch), BF16),
            pltpu.VMEM(block, BF16),
            pltpu.VMEM((windows, 8, frames), F32),
            pltpu.VMEM(block, BF16),
            pltpu.VMEM(block, F32),
            pltpu.VMEM(block, F32),
            pltpu.VMEM((2,) + block, F32),
            pltpu.VMEM(block, F32),
            pltpu.VMEM((3,) + block, BF16),
            pltpu.VMEM((windows + 2, frames, ch), BF16),
            pltpu.VMEM(block, BF16),
            pltpu.VMEM(block, BF16),
            pltpu.VMEM((2,) + block, BF16),
            pltpu.VMEM((windows, frames + frames // 2, ch), BF16),
            pltpu.VMEM((sum_rows, ch), F32),
            pltpu.VMEM((sum_rows, ch), BF16),
            pltpu.VMEM((sum_rows, ch), BF16),
            pltpu.VMEM(weights.shape, BF16),
            pltpu.SemaphoreType.DMA((52,)),
            pltpu.SemaphoreType.DMA((52,)),
            pltpu.SemaphoreType.DMA((2,)),
            pltpu.SemaphoreType.DMA((len(UNITS), 18)),
            pltpu.SemaphoreType.DMA((len(UNITS), 18)),
        ],
        compiler_params=pltpu.CompilerParams(
            collective_id=0, has_side_effects=True, vmem_limit_bytes=48 * 1024 * 1024
        ),
    )(frames_in, weights, biases, keep, cotangent)
    factor = 1.0 / math.sqrt(windows * frames * lax.axis_size("tlo") * lax.axis_size("thi"))
    scaled = sums.astype(F32) * factor
    weight_grad = jnp.pad(scaled[BIAS_ROWS:], ((0, 2 * ch), (0, 0)))
    bias_grad = scaled[: 8 * levels].reshape(levels, 8, ch)[:, 0]
    return (grad_in, weight_grad.reshape(levels, 3, ch, ch), bias_grad)


def shifted(block, axis, distance):
    devices = range(lax.axis_size(axis))
    route = [((i - distance) % len(devices), i) for i in devices]
    return lax.ppermute(block, axis, route)


def from_behind(value, axis, steps):
    count = lax.axis_size(axis)
    first, last = (max(0, -steps), min(count, count - steps))
    return lax.ppermute(value, axis, [(source, source + steps) for source in range(first, last)])


def smooth(values):
    return jax.nn.gelu(values, approximate=True)


def shift_shards(values, count):
    inner_size = lax.axis_size("tlo")
    outer_size = lax.axis_size("thi")
    if abs(count) >= inner_size * outer_size:
        return jnp.zeros_like(values)
    outer_by, inner_by = divmod(count, inner_size)
    rolled = values if inner_by == 0 else shifted(values, "tlo", inner_by)
    nearer = rolled if outer_by == 0 else from_behind(rolled, "thi", outer_by)
    if inner_by == 0:
        return nearer
    farther = rolled if outer_by + 1 == 0 else from_behind(rolled, "thi", outer_by + 1)
    return jnp.where(lax.axis_index("tlo") < inner_by, farther, nearer)


def tap_pair(values, dilation, sign):
    frames_dev = values.shape[1]
    if dilation < frames_dev:
        if sign > 0:
            edge = shift_shards(values[:, frames_dev - 2 * dilation :, :], 1)
            joined = jnp.concatenate([edge, values], axis=1)
            return (joined[:, dilation : dilation + frames_dev], joined[:, :frames_dev])
        edge = shift_shards(values[:, : 2 * dilation, :], -1)
        joined = jnp.concatenate([values, edge], axis=1)
        return (
            joined[:, dilation : dilation + frames_dev],
            joined[:, 2 * dilation : 2 * dilation + frames_dev],
        )
    hop_count = sign * (dilation // frames_dev)
    first = shift_shards(values, hop_count)
    second = shift_shards(values, 2 * hop_count)
    return (first, second)


def reduce_grads(weight_part, bias_part):
    return lax.psum((weight_part, bias_part), ("tlo", "thi"))


def shards(frames_in, weights, biases, valid_mask, cotangent):
    windows, frames_dev, channels = frames_in.shape
    widths = 3 * channels
    levels = weights.shape[0]
    keep = valid_mask.astype(jnp.float32)[:, :, None]
    dilations = [frames_dev // 4, frames_dev, 8 * frames_dev, 32 * frames_dev]
    current = frames_in
    saved = []
    for level in range(levels):
        first, second = tap_pair(current, dilations[level], 1)
        stacked = jnp.concatenate([current, first, second], axis=2).reshape(
            windows * frames_dev, widths
        )
        pre = (
            jnp.dot(
                stacked,
                weights[level].reshape(widths, channels),
                preferred_element_type=jnp.float32,
            )
            + biases[level]
        )
        pre = pre.reshape(windows, frames_dev, channels)
        current = (keep * (current.astype(jnp.float32) + smooth(pre))).astype(jnp.bfloat16)
        saved.append((stacked, pre))
    upstream = cotangent
    pending_weight = [None] * levels
    pending_bias = [None] * levels
    for level in reversed(range(levels)):
        stacked, pre = saved[level]
        through = upstream.astype(jnp.float32) * keep
        pull = jax.vjp(smooth, pre)[1]
        pre_grad = pull(through)[0].astype(jnp.bfloat16)
        flat_grad = pre_grad.reshape(windows * frames_dev, channels)
        weight_part = jnp.einsum(
            "rk,rc->kc", stacked, flat_grad, preferred_element_type=jnp.float32
        )
        bias_part = jnp.sum(flat_grad.astype(jnp.float32), axis=0)
        pending_weight[level] = weight_part
        pending_bias[level] = bias_part
        first, second = tap_pair(pre_grad, dilations[level], -1)
        gathered = jnp.concatenate([pre_grad, first, second], axis=2).reshape(
            windows * frames_dev, widths
        )
        mirrored = jnp.transpose(weights[level], (0, 2, 1)).reshape(widths, channels)
        back = jnp.dot(gathered, mirrored, preferred_element_type=jnp.float32).reshape(
            windows, frames_dev, channels
        )
        upstream = (through + back).astype(jnp.bfloat16)
    totals = reduce_grads(jnp.stack(pending_weight), jnp.stack(pending_bias))
    weight_sum = totals[0]
    bias_sum = totals[1]
    factor = 1.0 / math.sqrt(windows * frames_dev * lax.axis_size("tlo") * lax.axis_size("thi"))
    weight_grad = (weight_sum * factor).reshape(levels, 3, channels, channels)
    bias_grad = bias_sum * factor
    return (upstream, weight_grad, bias_grad)


def solution(mesh):
    fused = mesh.shape["tlo"] == 2 and mesh.shape["thi"] == 16
    return jax.shard_map(
        fused_shards if fused else shards,
        mesh=mesh,
        in_specs=(
            P(None, ("thi", "tlo"), None),
            P(),
            P(),
            P(None, ("thi", "tlo")),
            P(None, ("thi", "tlo"), None),
        ),
        out_specs=(P(None, ("thi", "tlo"), None), P(), P()),
        check_vma=False,
    )
```

```python
import math

import jax
import jax.numpy as jnp
from jax import lax
from jax.experimental import pallas as pl
from jax.experimental.pallas import tpu as pltpu
from jax.sharding import PartitionSpec as P

MESH = pl.DeviceIdType.MESH
F32 = jnp.float32
BF16 = jnp.bfloat16
UNITS = ((0, 1024), (1024, 512), (1536, 1024), (2560, 1536))
SUM_ROWS = 4096
BIAS_ROWS = 256


def rows_times(a, b):
    return jnp.dot(a, b, preferred_element_type=F32)


def rows_times_t(a, b):
    return lax.dot_general(a, b, (((1,), (1,)), ((), ())), preferred_element_type=F32)


def t_times_rows(a, b):
    return lax.dot_general(a, b, (((0,), (0,)), ((), ())), preferred_element_type=F32)


def gelu_and_slope(v):
    root = math.sqrt(2.0 / math.pi)
    square = v * v
    t = jnp.tanh(root * (v + 0.044715 * (square * v)))
    half = 0.5 * (1.0 + t)
    slope = half + (0.5 * v) * (1.0 - t * t) * (root * (1.0 + (3.0 * 0.044715) * square))
    return v * half, slope


def fused_kernel(
    x_ref, w_hbm, b_ref, keep_ref, cot_ref,
    out_ref, sum_ref,
    edge0, act1, prev1, act2, turned2, turned_cot, turned_keep, act3, own_wide, turned_wide,
    slope, through, grad, grad2, up_out, up2, next1, edge_back,
    acc, stage_send, stage_recv, w_ref,
    send_sem, recv_sem, local_sem, sum_send_sem, sum_recv_sem,
):
    windows, frames, ch = x_ref.shape
    rows = windows * frames
    y = lax.axis_index("tlo")
    thi = lax.axis_index("thi")
    block = thi * 2 + y
    z = thi // 4
    cx = lax.rem(thi, 4)
    xx = cx // 2
    core = lax.rem(thi, 2)

    near_z = z + 1 - 2 * lax.rem(z, 2)
    far_z = lax.rem(z + 2, 4)
    others = (far_z, 3 - z, near_z)

    def at_block(offset):
        other = lax.rem(block + offset + 32, 32)
        return (lax.rem(other, 2), other // 2)

    def at_z(other):
        return (y, other * 4 + cx)

    plane = {
        1: (1 - y, thi),
        2: (y, z * 4 + (1 - xx) * 2 + core),
        3: (1 - y, z * 4 + (1 - xx) * 2 + core),
    }
    plane_member = {
        1: xx * 2 + (1 - y),
        2: (1 - xx) * 2 + y,
        3: (1 - xx) * 2 + (1 - y),
    }
    z_member = {1: near_z, 2: far_z, 3: 3 - z}
    sibling = (y, z * 4 + xx * 2 + (1 - core))

    load_w = pltpu.make_async_copy(w_hbm, w_ref, local_sem.at[0])
    load_w.start()
    load_cot = pltpu.make_async_copy(cot_ref.at[z], turned_cot.at[z], local_sem.at[1])
    load_cot.start()
    barrier = pltpu.get_barrier_semaphore()
    greeted = [at_block(o) for o in (1, -1, 2, -2)]
    greeted += [at_z(other) for other in others]
    greeted += [sibling, plane[1], plane[2], plane[3]]
    for device in greeted:
        pl.semaphore_signal(barrier, inc=1, device_id=device, device_id_type=MESH)

    pending = []

    def send(src, dst, index, device):
        copy = pltpu.make_async_remote_copy(
            src_ref=src, dst_ref=dst, send_sem=send_sem.at[index], recv_sem=recv_sem.at[index],
            device_id=device, device_id_type=MESH,
        )
        copy.start()
        pending.append(copy)
        return copy

    half = frames // 2
    quarter = frames // 4
    pl.semaphore_wait(barrier, len(greeted))

    order = others + (z,)
    edge_copies = [
        send(x_ref.at[w, half:, :], edge0.at[w, :half, :], w, at_block(1)) for w in order
    ]
    keep_copies = [
        send(keep_ref.at[o], turned_keep.at[z], 40 + i, at_z(o)) for i, o in enumerate(others)
    ]
    cot_copies = [
        send(cot_ref.at[o], turned_cot.at[z], 43 + i, at_z(o)) for i, o in enumerate(others)
    ]
    turned_keep[z] = keep_ref[z]
    zeros = jnp.zeros((frames, ch), BF16)
    turned2[0] = zeros
    turned2[1] = zeros
    grad2[4] = zeros
    grad2[5] = zeros
    acc[:BIAS_ROWS, :] = jnp.zeros((BIAS_ROWS, ch), F32)
    edge0[:, half:, :] = x_ref[...]
    bias = b_ref[...]
    across = lax.broadcasted_iota(jnp.int32, (frames, frames), 0) == lax.broadcasted_iota(
        jnp.int32, (frames, frames), 1
    )
    ones = jnp.ones((frames, ch), BF16)

    def widen(row):
        diagonal = jnp.where(across, jnp.broadcast_to(row, (frames, frames)), 0.0)
        return rows_times(diagonal.astype(BF16), ones)

    for w in range(windows):
        own_wide[w] = widen(keep_ref[w, 0:1, :])

    def taps(level, a, b, c):
        total = rows_times(a, w_ref[level, 0]) + rows_times(b, w_ref[level, 1])
        return total + rows_times(c, w_ref[level, 2])

    def taps_back(level, a, b, c):
        total = rows_times_t(a, w_ref[level, 0]) + rows_times_t(b, w_ref[level, 1])
        return total + rows_times_t(c, w_ref[level, 2])

    load_w.wait()
    load_cot.wait()
    one_copies, two_copies = [], []
    for w, copy in zip(order, edge_copies):
        copy.wait_recv()

        @pl.when(block == 0)
        def _():
            edge0[w, :half, :] = jnp.zeros((half, ch), BF16)

        now = x_ref[w]
        total = taps(0, now, edge0[w, quarter : quarter + frames], edge0[w, 0:frames])
        gelu, d = gelu_and_slope(total + bias[0:1])
        slope[0, w] = d
        act1[w] = (own_wide[w] * (now.astype(F32) + gelu)).astype(BF16)
        one_copies.append(send(act1.at[w], prev1.at[0, w], 4 + w, at_block(1)))
        two_copies.append(send(act1.at[w], prev1.at[1, w], 8 + w, at_block(2)))

    act_copies = []
    for i, w in enumerate(order):
        one_copies[i].wait_recv()
        two_copies[i].wait_recv()

        @pl.when(block < 1)
        def _():
            prev1[0, w] = zeros

        @pl.when(block < 2)
        def _():
            prev1[1, w] = zeros

        now = act1[w]
        total = taps(1, now, prev1[0, w], prev1[1, w])
        gelu, d = gelu_and_slope(total + bias[1:2])
        slope[1, w] = d
        result = (own_wide[w] * (now.astype(F32) + gelu)).astype(BF16)
        if i < 3:
            act2[w] = result
            act_copies.append(send(act2.at[w], turned2.at[2 + z], 46 + i, at_z(w)))
        else:
            turned2[2 + z] = result

    for copy in keep_copies:
        copy.wait_recv()
    for w in range(windows):
        turned_wide[w] = widen(turned_keep[w, 0:1, :])
    for copy in cot_copies + act_copies:
        copy.wait_recv()

    def flat(ref, first):
        return ref[pl.ds(first, 2)].reshape(2 * frames, ch)

    def put(ref, first, value):
        ref[pl.ds(first, 2)] = value.reshape(2, frames, ch)

    def add_bias(level, g):
        at = 8 * level
        acc[at : at + 1, :] += jnp.sum(g.astype(F32), axis=0, keepdims=True)

    def far_levels(i, _):
        first = 2 * i
        now = flat(turned2, 2 + first)
        keep = flat(turned_wide, first)
        total = taps(2, now, flat(turned2, 1 + first), flat(turned2, first))
        gelu, d = gelu_and_slope(total + bias[2:3])
        last = (keep * (now.astype(F32) + gelu)).astype(BF16)
        put(act3, first, last)
        _, d3 = gelu_and_slope(rows_times(last, w_ref[3, 0]) + bias[3:4])
        t = keep * flat(turned_cot, first).astype(F32)
        g = (t * d3).astype(BF16)
        grad[0, pl.ds(first, 2)] = g.reshape(2, frames, ch)
        add_bias(3, g)
        t = keep * (t + rows_times_t(g, w_ref[3, 0])).astype(BF16).astype(F32)
        g = (t * d).astype(BF16)
        put(grad2, first, g)
        put(through, first, t)
        add_bias(2, g)
        return 0

    lax.fori_loop(0, 2, far_levels, 0)

    up_copies = []
    for i, w in enumerate(order):
        result = through[w] + taps_back(2, grad2[w], grad2[w + 1], grad2[w + 2])
        if i < 3:
            up_out[w] = result.astype(BF16)
            up_copies.append(send(up_out.at[w], up2.at[z], 49 + i, at_z(w)))
        else:
            up2[z] = result.astype(BF16)

    def put_weight(slot, a, g):
        acc[BIAS_ROWS + slot * ch : BIAS_ROWS + (slot + 1) * ch, :] = t_times_rows(a, g)

    def plan(base, size):
        half_at = base + core * (size // 2)
        n = size // 8
        mine = xx * 2 + y
        part = half_at + mine * n
        first = [(sibling, base + (1 - core) * (size // 2), base)]
        second = [
            (plane[r], half_at + plane_member[r] * n, base + size // 2 + (r - 1) * n) for r in (1, 2, 3)
        ]
        m = size // 32
        landed = base + size // 2 + 3 * n
        third = [
            (at_z(z_member[r]), part + z_member[r] * m, landed + (r - 1) * m) for r in (1, 2, 3)
        ]
        return (
            (first, half_at, size // 2),
            (second, part, n),
            (third, part + z * m, m),
        )

    plans = [plan(*unit) for unit in UNITS]
    flying = {}

    def aligned(at, n):
        return pl.ds(at if isinstance(at, int) else pl.multiple_of(at, 16), n)

    def sum_copy(src, dst, unit, index, device):
        copy = pltpu.make_async_remote_copy(
            src_ref=src, dst_ref=dst, send_sem=sum_send_sem.at[unit, index],
            recv_sem=sum_recv_sem.at[unit, index], device_id=device, device_id_type=MESH,
        )
        copy.start()
        pending.append(copy)
        return copy

    def begin(unit, stage):
        copies = []
        routes, own, n = plans[unit][stage if stage < 3 else 5 - stage]
        span = aligned(own, n)
        if stage == 3:
            sum_ref[span, :] = acc[span, :].astype(BF16)
        for r, (device, give, landing) in enumerate(routes):
            if stage < 3:
                there = aligned(give, n)
                stage_send[there, :] = acc[there, :].astype(BF16)
                src, dst = stage_send.at[there, :], stage_recv.at[pl.ds(landing, n), :]
            else:
                src, dst = sum_ref.at[span, :], sum_ref.at[span, :]
            copies.append(sum_copy(src, dst, unit, 3 * stage + r, device))
        flying[unit, stage] = copies

    def finish(unit, stage):
        for copy in flying[unit, stage]:
            copy.wait_recv()
        if stage < 3:
            routes, own, n = plans[unit][stage]
            span = aligned(own, n)
            total = acc[span, :]
            for _, _, landing in routes:
                total = total + stage_recv[landing : landing + n, :].astype(F32)
            acc[span, :] = total

    def advance(unit, stage):
        if stage > 0:
            finish(unit, stage - 1)
        if stage < 6:
            begin(unit, stage)

    back_order = (z, near_z, far_z, 3 - z)
    arrivals = (None, up_copies[2], up_copies[0], up_copies[1])
    back_one, back_two = [], []

    def start_one(i):
        w = back_order[i]
        if i > 0:
            arrivals[i].wait_recv()
        t = own_wide[w] * up2[w].astype(F32)
        g = (t * slope[1, w]).astype(BF16)
        through[w] = t
        grad[1, w] = g
        back_one.append(send(grad.at[1, w], next1.at[0, w], 12 + w, at_block(-1)))
        back_two.append(send(grad.at[1, w], next1.at[1, w], 16 + w, at_block(-2)))
        add_bias(1, g)

    start_one(0)
    put_weight(9, act3[...].reshape(rows, ch), grad[0].reshape(rows, ch))
    for tap in range(3):
        n = 4 - tap
        put_weight(6 + tap, turned2[2 : 2 + n].reshape(n * frames, ch), grad2[tap:4].reshape(n * frames, ch))
    advance(3, 0)
    for i in range(1, 4):
        start_one(i)
    advance(3, 1)
    g1 = grad[1].reshape(rows, ch)
    put_weight(3, act1[...].reshape(rows, ch), g1)
    put_weight(4, prev1[0].reshape(rows, ch), g1)
    put_weight(5, prev1[1].reshape(rows, ch), g1)
    advance(2, 0)
    advance(3, 2)
    back_edges = []
    for i, w in enumerate(back_order):
        back_one[i].wait_recv()
        back_two[i].wait_recv()

        @pl.when(block >= 31)
        def _():
            next1[0, w] = zeros

        @pl.when(block >= 30)
        def _():
            next1[1, w] = zeros

        total = through[w] + taps_back(1, grad[1, w], next1[0, w], next1[1, w])
        t = own_wide[w] * total.astype(BF16).astype(F32)
        g = (t * slope[0, w]).astype(BF16)
        through[w] = t
        grad[2, w] = g
        edge_back[w, :frames, :] = g
        back_edges.append(
            send(grad.at[2, w, :half, :], edge_back.at[w, frames:, :], 20 + w, at_block(-1))
        )
        add_bias(0, g)
    advance(2, 1)
    advance(3, 3)
    g0 = grad[2].reshape(rows, ch)
    put_weight(0, x_ref[...].reshape(rows, ch), g0)
    put_weight(1, edge0[:, quarter : quarter + frames].reshape(rows, ch), g0)
    advance(0, 0)
    put_weight(2, edge0[:, 0:frames].reshape(rows, ch), g0)
    advance(1, 0)
    advance(2, 2)
    advance(0, 1)
    advance(1, 1)
    advance(3, 4)
    for i, w in enumerate(back_order):
        back_edges[i].wait_recv()

        @pl.when(block >= 31)
        def _():
            edge_back[w, frames:, :] = jnp.zeros((half, ch), BF16)

        total = through[w] + taps_back(
            0, grad[2, w], edge_back[w, quarter : quarter + frames], edge_back[w, half : half + frames]
        )
        out_ref[w] = total.astype(BF16)
    at = [1, 1, 2, 4]
    while min(at) < 6:
        for u in range(len(UNITS)):
            if at[u] < 6:
                at[u] += 1
                advance(u, at[u])
    for copy in pending:
        copy.wait_send()


def fused_shards(frames_in, weights, biases, valid_mask, cotangent):
    windows, frames, ch = frames_in.shape
    levels = weights.shape[0]
    keep = jnp.broadcast_to(valid_mask.astype(F32)[:, None, :], (windows, 8, frames))
    vmem = pl.BlockSpec(memory_space=pltpu.VMEM)
    anywhere = pl.BlockSpec(memory_space=pl.ANY)
    block = (windows, frames, ch)
    sum_rows = SUM_ROWS
    grad_in, sums = pl.pallas_call(
        fused_kernel,
        out_shape=(
            jax.ShapeDtypeStruct(block, BF16),
            jax.ShapeDtypeStruct((sum_rows, ch), BF16),
        ),
        in_specs=[vmem, anywhere, vmem, vmem, anywhere],
        out_specs=(vmem, vmem),
        scratch_shapes=[
            pltpu.VMEM((windows, frames + frames // 2, ch), BF16),
            pltpu.VMEM(block, BF16),
            pltpu.VMEM((2,) + block, BF16),
            pltpu.VMEM(block, BF16),
            pltpu.VMEM((windows + 2, frames, ch), BF16),
            pltpu.VMEM(block, BF16),
            pltpu.VMEM((windows, 8, frames), F32),
            pltpu.VMEM(block, BF16),
            pltpu.VMEM(block, F32),
            pltpu.VMEM(block, F32),
            pltpu.VMEM((2,) + block, F32),
            pltpu.VMEM(block, F32),
            pltpu.VMEM((3,) + block, BF16),
            pltpu.VMEM((windows + 2, frames, ch), BF16),
            pltpu.VMEM(block, BF16),
            pltpu.VMEM(block, BF16),
            pltpu.VMEM((2,) + block, BF16),
            pltpu.VMEM((windows, frames + frames // 2, ch), BF16),
            pltpu.VMEM((sum_rows, ch), F32),
            pltpu.VMEM((sum_rows, ch), BF16),
            pltpu.VMEM((sum_rows, ch), BF16),
            pltpu.VMEM(weights.shape, BF16),
            pltpu.SemaphoreType.DMA((52,)),
            pltpu.SemaphoreType.DMA((52,)),
            pltpu.SemaphoreType.DMA((2,)),
            pltpu.SemaphoreType.DMA((len(UNITS), 18)),
            pltpu.SemaphoreType.DMA((len(UNITS), 18)),
        ],
        compiler_params=pltpu.CompilerParams(
            collective_id=0, has_side_effects=True, vmem_limit_bytes=48 * 1024 * 1024
        ),
    )(frames_in, weights, biases, keep, cotangent)
    factor = 1.0 / math.sqrt(windows * frames * lax.axis_size("tlo") * lax.axis_size("thi"))
    scaled = sums.astype(F32) * factor
    none = jnp.zeros((2, ch, ch), F32)
    grads = scaled[BIAS_ROWS:].reshape(10, ch, ch)
    weight_grad = jnp.concatenate([grads[0:3], grads[3:6], grads[6:9], grads[9:10], none])
    bias_grad = scaled[: 8 * levels].reshape(levels, 8, ch)[:, 0]
    return (grad_in, weight_grad.reshape(levels, 3, ch, ch), bias_grad)


def shifted(block, axis, distance):
    devices = range(lax.axis_size(axis))
    route = [((i - distance) % len(devices), i) for i in devices]
    return lax.ppermute(block, axis, route)


def from_behind(value, axis, steps):
    count = lax.axis_size(axis)
    first, last = (max(0, -steps), min(count, count - steps))
    return lax.ppermute(value, axis, [(source, source + steps) for source in range(first, last)])


def smooth(values):
    return jax.nn.gelu(values, approximate=True)


def shift_shards(values, count):
    inner_size = lax.axis_size("tlo")
    outer_size = lax.axis_size("thi")
    if abs(count) >= inner_size * outer_size:
        return jnp.zeros_like(values)
    outer_by, inner_by = divmod(count, inner_size)
    rolled = values if inner_by == 0 else shifted(values, "tlo", inner_by)
    nearer = rolled if outer_by == 0 else from_behind(rolled, "thi", outer_by)
    if inner_by == 0:
        return nearer
    farther = rolled if outer_by + 1 == 0 else from_behind(rolled, "thi", outer_by + 1)
    return jnp.where(lax.axis_index("tlo") < inner_by, farther, nearer)


def tap_pair(values, dilation, sign):
    frames_dev = values.shape[1]
    if dilation < frames_dev:
        if sign > 0:
            edge = shift_shards(values[:, frames_dev - 2 * dilation :, :], 1)
            joined = jnp.concatenate([edge, values], axis=1)
            return (joined[:, dilation : dilation + frames_dev], joined[:, :frames_dev])
        edge = shift_shards(values[:, : 2 * dilation, :], -1)
        joined = jnp.concatenate([values, edge], axis=1)
        return (
            joined[:, dilation : dilation + frames_dev],
            joined[:, 2 * dilation : 2 * dilation + frames_dev],
        )
    hop_count = sign * (dilation // frames_dev)
    first = shift_shards(values, hop_count)
    second = shift_shards(values, 2 * hop_count)
    return (first, second)


def reduce_grads(weight_part, bias_part):
    return lax.psum((weight_part, bias_part), ("tlo", "thi"))


def shards(frames_in, weights, biases, valid_mask, cotangent):
    windows, frames_dev, channels = frames_in.shape
    widths = 3 * channels
    levels = weights.shape[0]
    keep = valid_mask.astype(jnp.float32)[:, :, None]
    dilations = [frames_dev // 4, frames_dev, 8 * frames_dev, 32 * frames_dev]
    current = frames_in
    saved = []
    for level in range(levels):
        first, second = tap_pair(current, dilations[level], 1)
        stacked = jnp.concatenate([current, first, second], axis=2).reshape(
            windows * frames_dev, widths
        )
        pre = (
            jnp.dot(
                stacked,
                weights[level].reshape(widths, channels),
                preferred_element_type=jnp.float32,
            )
            + biases[level]
        )
        pre = pre.reshape(windows, frames_dev, channels)
        current = (keep * (current.astype(jnp.float32) + smooth(pre))).astype(jnp.bfloat16)
        saved.append((stacked, pre))
    upstream = cotangent
    pending_weight = [None] * levels
    pending_bias = [None] * levels
    for level in reversed(range(levels)):
        stacked, pre = saved[level]
        through = upstream.astype(jnp.float32) * keep
        pull = jax.vjp(smooth, pre)[1]
        pre_grad = pull(through)[0].astype(jnp.bfloat16)
        flat_grad = pre_grad.reshape(windows * frames_dev, channels)
        weight_part = jnp.einsum(
            "rk,rc->kc", stacked, flat_grad, preferred_element_type=jnp.float32
        )
        bias_part = jnp.sum(flat_grad.astype(jnp.float32), axis=0)
        pending_weight[level] = weight_part
        pending_bias[level] = bias_part
        first, second = tap_pair(pre_grad, dilations[level], -1)
        gathered = jnp.concatenate([pre_grad, first, second], axis=2).reshape(
            windows * frames_dev, widths
        )
        mirrored = jnp.transpose(weights[level], (0, 2, 1)).reshape(widths, channels)
        back = jnp.dot(gathered, mirrored, preferred_element_type=jnp.float32).reshape(
            windows, frames_dev, channels
        )
        upstream = (through + back).astype(jnp.bfloat16)
    totals = reduce_grads(jnp.stack(pending_weight), jnp.stack(pending_bias))
    weight_sum = totals[0]
    bias_sum = totals[1]
    factor = 1.0 / math.sqrt(windows * frames_dev * lax.axis_size("tlo") * lax.axis_size("thi"))
    weight_grad = (weight_sum * factor).reshape(levels, 3, channels, channels)
    bias_grad = bias_sum * factor
    return (upstream, weight_grad, bias_grad)


def solution(mesh):
    fused = mesh.shape["tlo"] == 2 and mesh.shape["thi"] == 16
    return jax.shard_map(
        fused_shards if fused else shards,
        mesh=mesh,
        in_specs=(
            P(None, ("thi", "tlo"), None),
            P(),
            P(),
            P(None, ("thi", "tlo")),
            P(None, ("thi", "tlo"), None),
        ),
        out_specs=(P(None, ("thi", "tlo"), None), P(), P()),
        check_vma=False,
    )
```
